32 devices in a mesh: seq: 8 (over z, y), tensor: 4 (over x, core).
Axes of the slice: x: 2, y: 2, z: 4, core: 2. Of those that a mesh axis runs over, the one named last changes fastest.
Arguments:
- query: bfloat16 [1024, 2048], P('seq', 'tensor')
- suffix_kv: bfloat16 [1024, 4, 2, 128], P('seq'), may hold values from -6 to 6
- segment_ids: int32 [8, 128], P('seq'), may hold values from 0 to 3, never falling along the last dimension, each value on 1 to 64 neighbouring positions
- request_prefix: int32 [8, 4], P('seq'), may hold values from 0 to 3
- prefix_kv: bfloat16 [8192, 4, 2, 128], P('seq')
- shard_prefix: int32 [8], P('seq'), may hold values from 0 to 3, as said below
- residual: bfloat16 [1024, 2048], P('seq'), may hold values from -3.2 to 3.2
- out_weight: bfloat16 [2048, 2048], P('tensor'), may hold values from -0.1875 to 0.1875
- norm_gain: float32 [2048], replicated, may hold values from 0.1 to 1.9
- expert_ids: int32 [1024, 6], P('seq'), may hold values from 0 to 15, all different within a row; in each aligned block of 128 rows (0 to 127, 128 to 255, ...) at most 96 rows name the same one
- gate_weights: float32 [1024, 6], P('seq'), may hold values from 0.05 to 0.5
- expert_in: bfloat16 [16, 2048, 2, 1408], P('seq', None, None, 'tensor'), may hold values from -0.125 to 0.125
- expert_out: bfloat16 [16, 1408, 2048], P('seq', 'tensor'), may hold values from -0.21875 to 0.21875
Outputs:
- attended: bfloat16 [1024, 2048], P('seq', 'tensor')
- layer_out: bfloat16 [1024, 2048], P('seq', 'tensor')
The draws below stay inside these ranges and needn't reach their ends.
Inputs may be any that keep to these rules, and one draw needn't show every extreme that they name: `segment_ids`: on each seq index the segment numbers never fall along the 128 positions and every number occurs. `shard_prefix`: every prefix owns the same number of shards. `expert_ids`: each row names 6 different experts; within the 128 rows of one seq index no expert is named more than 96 times, and that count is reached.
All inputs are finite; a program needn't handle non-finite values.
Results may differ from the reference program's by a relative error of at most 0.02.
Values may be sent and summed in bfloat16 or wider, within the bound.
A program may use at most 128 MiB of HBM per device.

```python
import math
import jax
import jax.numpy as jnp
import numpy as np
from jax import lax

D = 2048
QH = 16
KVH = 4
HD = 128
MOE_FF = 1408
TOP = 6
PREFIXES = 4
REQ_DEV = 4
TOK_DEV = 128
PSH = 1024
TOKENS = 1024
PREF_TOTAL = 8192
EXPERTS = 16
CAP = 96
HID_GROUP = 352
N_SEQ = 8
N_TENSOR = 4


def draw_query(key, part):
    shape = (TOKENS, QH * HD)
    base = jnp.clip(2.0 * jax.random.normal(jax.random.fold_in(key, 1), shape, jnp.float32), -8.0, 8.0)
    return base.astype(jnp.bfloat16)


def draw_prefix_kv(key, part):
    shape = (PREF_TOTAL, KVH, 2, HD)
    base = jnp.clip(jax.random.normal(jax.random.fold_in(key, 2), shape, jnp.float32), -6.0, 6.0)
    return base.astype(jnp.bfloat16)


def draw_shard_prefix(key, part):
    shard_total = PREF_TOTAL // PSH
    order = jax.random.permutation(jax.random.fold_in(key, 3), shard_total)
    return (order // (shard_total // PREFIXES)).astype(jnp.int32)


def draw_residual(key, part):
    shape = (TOKENS, D)
    columns = jnp.arange(D).astype(jnp.float32) / D
    scale = 0.08 * 10.0 ** columns
    base = jnp.clip(jax.random.normal(jax.random.fold_in(key, 5), shape, jnp.float32), -4.0, 4.0)
    return (base * scale[None, :]).astype(jnp.bfloat16)


def set_ends(entries, stream_key, low, high):
    spot = [jax.random.randint(jax.random.fold_in(stream_key, axis), (), 0, length) for axis, length in enumerate(entries.shape)]
    main_axis = entries.shape.index(max(entries.shape))
    neighbour = spot[:main_axis] + [(spot[main_axis] + 1) % entries.shape[main_axis]] + spot[main_axis + 1:]
    return entries.at[tuple(spot)].set(low).at[tuple(neighbour)].set(high)


def strengthened(values, stream_key, source, target, blocks, factor):
    def block_of(dim):
        return (jnp.arange(values.shape[dim]) // (values.shape[dim] // blocks)).reshape((-1,) + (1,) * (values.ndim - 1 - dim))

    first = jax.random.permutation(stream_key, blocks)[block_of(target)]
    second = (block_of(target) + blocks // 2) % blocks
    return jnp.where((block_of(source) == first) | (block_of(source) == second), factor * values, values)


def block_levels(rng, shape, pieces, low, high):
    def one(axis_at, shards_of):
        steps = jax.random.uniform(jax.random.fold_in(jax.random.fold_in(rng, 6), axis_at), (shards_of,), jnp.float32, low / len(pieces), high / len(pieces))
        return jnp.repeat(jnp.exp(steps), shape[axis_at] // shards_of).reshape((-1,) + (1,) * (len(shape) - axis_at - 1))

    gain = one(*pieces[0])
    for cut in pieces[1:]:
        gain = gain * one(*cut)
    return gain


def rank_bounds(number_of, lean):
    loads = [(1 << 20) // math.isqrt(standing ** lean) + 1 for standing in range(1, number_of + 1)]
    deviation = 1 + sum(loads) // (1 << 30)
    return np.cumsum(np.array([max(1, weight // deviation) for weight in loads]))


def skewed_ids(stream_key, dims, number_of, lean):
    table = rank_bounds(number_of, lean)
    ticket = jax.random.randint(jax.random.fold_in(stream_key, 1), dims, 0, int(table[number_of - 1]))
    grade = jnp.searchsorted(jnp.asarray(table, jnp.int32), ticket, side="right")
    return jax.random.permutation(jax.random.fold_in(stream_key, 2), number_of)[grade].astype(jnp.int32)


def length_profile(amount, total, most, slope):
    loads = [(1 << 20) // math.isqrt(grade ** slope) + 1 for grade in range(2, amount + 1)]
    surplus, given = total - most - (amount - 1), [1] * (amount - 1)
    while surplus > 0:
        free = [i for i in range(amount - 1) if given[i] < most]
        pool, remaining = sum([loads[i] for i in free]), surplus
        for i in free:
            more = min(most - given[i], max(1, remaining * loads[i] // pool), surplus)
            given[i] = given[i] + more
            surplus = surplus - more
    return np.array([most] + given)


def uneven_parts(stream_key, amount, total, most, slope):
    if amount == 2:
        one = jax.random.randint(stream_key, (), max(1, total - most), min(most, total - 1) + 1)
        return jnp.stack([one, total - one])
    sizes = jnp.asarray(length_profile(amount, total, most, slope), jnp.int32)
    twos = (amount - 1) // 2
    giver, sink = sizes[1:1 + 2 * twos:2], sizes[2:2 + 2 * twos:2]
    margin = jnp.minimum(giver - 1, most - sink)
    shifted = jax.random.randint(jax.random.fold_in(stream_key, 1), (twos,), 0, 1 << 20) % (margin + 1)
    sizes = sizes.at[1:1 + 2 * twos:2].set(giver - shifted).at[2:2 + 2 * twos:2].set(sink + shifted)
    return sizes[jax.random.permutation(jax.random.fold_in(stream_key, 2), amount)]


def routed_block(own_key, own, number, rows, amount, top, most, lean):
    order = jax.random.permutation(own_key, amount)
    crowded, common = shares(amount, rows * top, most, lean, True), shares(amount, rows * top, most, lean, False)
    places = jnp.arange(amount)

    def named(lengths, offset_by):
        used = int((lengths > 0).sum())
        fixed = max(1, used // 4)
        passed = fixed + (places - fixed + offset_by * (used - fixed)) % max(1, amount - fixed)
        return jnp.zeros((amount,), jnp.int32).at[order[jnp.where(places < fixed, places, passed)]].set(jnp.asarray(lengths, jnp.int32))

    lengths = jnp.where(number % 4 == 0, named(crowded, number // 4), named(common, number - number // 4 - 1))
    mixed = jax.random.permutation(jax.random.fold_in(own, 3), amount)
    source_of, sink = mixed[0:amount // 2 * 2:2], mixed[1:amount // 2 * 2:2]
    room = jnp.minimum(lengths[source_of] - 1, most - lengths[sink]) // 2
    room = jnp.where((source_of == order[0]) | (sink == order[0]) | (lengths[sink] == 0), 0, jnp.maximum(room, 0))
    passed = jax.random.randint(jax.random.fold_in(own, 4), (amount // 2,), 0, 1 << 20) % (room + 1)
    lengths = lengths.at[source_of].add(-passed).at[sink].add(passed)
    items = jnp.searchsorted(jnp.cumsum(lengths), jnp.arange(rows * top), side="right").astype(jnp.int32)
    listing = items.reshape(top, rows).T
    listing = listing[jax.random.permutation(jax.random.fold_in(own, 1), rows)]
    offset_by = jax.random.randint(jax.random.fold_in(own, 2), (rows, 1), 0, top)
    return jnp.take_along_axis(listing, (jnp.arange(top)[None, :] + offset_by) % top, axis=1)


def shares(amount, total, most, skew, full):
    weights = [(1 << 20) // math.isqrt(standing ** skew) + 1 for standing in range(1, amount + 1)]
    largest = most if full else min(most, max(-(-total // amount), total * weights[0] // sum(weights)))
    least = 1 if total - largest >= amount - 1 else 0
    given, spare = [largest] + [least] * (amount - 1), total - largest - least * (amount - 1)
    while spare > 0:
        candidates = [i for i in range(1, amount) if given[i] < largest] or [i for i in range(1, amount) if given[i] < most]
        pool, left = sum([weights[i] for i in candidates]), spare
        for i in candidates:
            more = min(most - given[i], max(1, left * weights[i] // pool), spare)
            given[i] = given[i] + more
            spare = spare - more
    return np.array(given)


def normal_values(key, extent, spread, bound, shards=(), held_as=jnp.bfloat16):
    values = jax.random.normal(key, extent, jnp.float32) * spread
    if len(shards) > 0:
        values = block_levels(key, extent, shards, -0.22, 0.18) * values
    return jnp.clip(values, min=-bound, max=bound).astype(held_as)


def bell_draw_with(rng, shape, scale, bound, pieces, heavy, kind=jnp.bfloat16):
    entries = scale * jax.random.normal(rng, shape, jnp.float32)
    if pieces:
        entries = entries * block_levels(rng, shape, pieces, -0.22, 0.18)
    return jnp.clip(strengthened(entries, jax.random.fold_in(rng, 3), *heavy), -bound, bound).astype(kind)


def setup_inputs(seed: int = 0) -> dict:
    arg_keys = jax.random.split(jax.random.key(seed), 14)
    query = draw_query(jax.random.fold_in(arg_keys[13], 71), 0)
    suffix_kv = normal_values(arg_keys[1], (TOKENS, KVH, 2, HD), 1.0, 6.0, ((0, 8),))
    segment_ids = jax.vmap(lambda own: jnp.searchsorted(jnp.cumsum(uneven_parts(own, REQ_DEV, TOK_DEV, TOK_DEV // 2, 1)), jnp.arange(TOK_DEV), side="right"))(jax.random.split(arg_keys[2], N_SEQ)).reshape((N_SEQ, TOK_DEV)).astype(jnp.int32)
    request_prefix = set_ends(skewed_ids(arg_keys[3], (N_SEQ, REQ_DEV), PREFIXES, 2), jax.random.fold_in(arg_keys[3], 3), 0, PREFIXES - 1).astype(jnp.int32)
    prefix_kv = draw_prefix_kv(jax.random.fold_in(arg_keys[13], 71), 0)
    shard_prefix = draw_shard_prefix(jax.random.fold_in(arg_keys[13], 71), 0)
    residual = draw_residual(jax.random.fold_in(arg_keys[13], 71), 0)
    out_weight = bell_draw_with(arg_keys[7], (QH * HD, D), (QH * HD) ** -0.5, 0.1875, ((0, 4),), (0, 1, 4, 2.0))
    norm_gain = jnp.clip(1.0 + 0.18 * jax.random.normal(arg_keys[8], (D,), jnp.float32), 0.1, 1.9)
    expert_ids_keys = jax.random.split(jax.random.fold_in(arg_keys[9], 1), TOKENS // TOK_DEV)
    expert_ids_turns = jax.random.permutation(jax.random.fold_in(arg_keys[9], 3), TOKENS // TOK_DEV)
    expert_ids = jax.vmap(lambda own, number: routed_block(jax.random.fold_in(arg_keys[9], 2), own, number, TOK_DEV, EXPERTS, TOP, CAP, 2))(expert_ids_keys, expert_ids_turns).reshape((TOKENS, TOP))
    gate_weights = jnp.clip(jnp.exp(math.log(0.5) - 2.3025851 * jax.random.uniform(arg_keys[10], (TOKENS, TOP), jnp.float32) ** block_levels(arg_keys[10], (TOKENS, TOP), ((0, 8),), -0.2, 0.2)), 0.05, 0.5)
    expert_in = normal_values(arg_keys[11], (EXPERTS, D, 2, MOE_FF), D ** -0.5, 0.125, ((0, 8), (3, 4)))
    expert_out = bell_draw_with(arg_keys[12], (EXPERTS, MOE_FF, D), MOE_FF ** -0.5, 0.21875, ((0, 8), (1, 4)), (1, 2, 4, 2.0))
    return dict(query=query, suffix_kv=suffix_kv, segment_ids=segment_ids, request_prefix=request_prefix, prefix_kv=prefix_kv, shard_prefix=shard_prefix, residual=residual, out_weight=out_weight, norm_gain=norm_gain, expert_ids=expert_ids, gate_weights=gate_weights, expert_in=expert_in, expert_out=expert_out)


PRECISE = lax.Precision.HIGHEST

def rounded(values):
    return lax.optimization_barrier(values.astype(jnp.bfloat16)).astype(jnp.float32)

def attend_device(device_item, prefix_kv, key_owner):
    queries, suffix_rows, segments, requests = device_item
    groups = QH // KVH
    query_f32 = queries.astype(jnp.float32).reshape(TOK_DEV, KVH, groups, HD)
    prefix_f32 = prefix_kv.astype(jnp.float32)
    suffix_f32 = suffix_rows.astype(jnp.float32)
    score_scale = HD ** (-0.5)
    row_prefix = requests[segments]
    prefix_scores = jnp.einsum('tkgd,pkd->kgtp', query_f32, prefix_f32[:, :, 0], precision=PRECISE) * score_scale
    visible = row_prefix[:, None] == key_owner[None, :]
    prefix_scores = jnp.where(visible[None, None], prefix_scores, -jnp.inf)
    positions = jnp.arange(TOK_DEV)
    causal = (segments[:, None] == segments[None, :]) & (positions[None, :] <= positions[:, None])
    suffix_scores = jnp.einsum('tkgd,skd->kgts', query_f32, suffix_f32[:, :, 0], precision=PRECISE) * score_scale
    suffix_scores = jnp.where(causal[None, None], suffix_scores, -jnp.inf)
    highest = jnp.maximum(lax.optimization_barrier(jnp.max(prefix_scores, axis=3)), lax.optimization_barrier(jnp.max(suffix_scores, axis=3)))
    prefix_weights = jnp.exp(prefix_scores - highest[..., None])
    suffix_weights = jnp.exp(suffix_scores - highest[..., None])
    denominator = lax.optimization_barrier(jnp.sum(prefix_weights, axis=3)) + lax.optimization_barrier(jnp.sum(suffix_weights, axis=3))
    combined = jnp.einsum('kgtp,pkd->tkgd', rounded(prefix_weights), prefix_f32[:, :, 1], precision=PRECISE)
    combined = combined + jnp.einsum('kgts,skd->tkgd', rounded(suffix_weights), suffix_f32[:, :, 1], precision=PRECISE)
    combined = combined / jnp.transpose(denominator, (2, 0, 1))[..., None]
    return combined.reshape(TOK_DEV, QH * HD).astype(jnp.bfloat16)

def run_expert(expert_item):
    rows_in, weight_in, weight_out = expert_item
    gate_up = jnp.dot(rows_in, weight_in.reshape(D, 2 * MOE_FF), preferred_element_type=jnp.float32)
    gate_up = gate_up.reshape(-1, 2, MOE_FF)
    hidden = (jax.nn.silu(gate_up[:, 0]) * gate_up[:, 1]).astype(jnp.bfloat16)
    grouped = jnp.einsum('rgh,ghd->grd', hidden.reshape(-1, N_TENSOR, HID_GROUP).astype(jnp.float32), weight_out.reshape(N_TENSOR, HID_GROUP, D).astype(jnp.float32), precision=PRECISE)
    grouped = lax.optimization_barrier(grouped.astype(jnp.bfloat16))
    return lax.optimization_barrier(jnp.sum(grouped.astype(jnp.float32), axis=0)).astype(jnp.bfloat16)

def reference(query, suffix_kv, segment_ids, request_prefix, prefix_kv, shard_prefix, residual, out_weight, norm_gain, expert_ids, gate_weights, expert_in, expert_out):
    key_owner = jnp.repeat(shard_prefix, PSH)

    def one_device(device_item):
        return attend_device(device_item, prefix_kv, key_owner)
    attention = lax.map(one_device, (query.reshape(N_SEQ, TOK_DEV, QH * HD), suffix_kv.reshape(N_SEQ, TOK_DEV, KVH, 2, HD), segment_ids, request_prefix))
    attention = attention.reshape(TOKENS, QH * HD)
    hidden_state = residual.astype(jnp.float32) + jnp.dot(attention, out_weight, preferred_element_type=jnp.float32)
    attended = hidden_state.astype(jnp.bfloat16)
    mean_square = lax.optimization_barrier(jnp.mean(hidden_state * hidden_state, axis=1, keepdims=True))
    normed = (hidden_state * lax.rsqrt(mean_square + 1e-06) * norm_gain.astype(jnp.float32)[None, :]).astype(jnp.bfloat16)
    flat_ids = expert_ids.reshape(N_SEQ, TOK_DEV * TOP).astype(jnp.int32)
    onehot = (flat_ids[:, :, None] == jnp.arange(EXPERTS, dtype=jnp.int32)[None, None, :]).astype(jnp.int32)
    slot_index = lax.optimization_barrier(jnp.sum((jnp.cumsum(onehot, axis=1) - 1) * onehot, axis=2)).astype(jnp.int32)
    sources = jnp.arange(N_SEQ, dtype=jnp.int32)[:, None]
    places = ((flat_ids * N_SEQ + sources) * CAP + slot_index).reshape(-1).astype(jnp.int32)
    table = jnp.zeros((EXPERTS * N_SEQ * CAP, D), jnp.bfloat16).at[places].set(jnp.repeat(normed, TOP, axis=0))
    table = table.reshape(EXPERTS, N_SEQ * CAP, D)
    outputs = lax.map(run_expert, (table, expert_in, expert_out))
    picked = outputs.reshape(EXPERTS * N_SEQ * CAP, D)[places].reshape(TOKENS, TOP, D)
    mixture = lax.optimization_barrier(jnp.sum(gate_weights[:, :, None] * picked.astype(jnp.float32), axis=1))
    layer_out = (hidden_state + mixture).astype(jnp.bfloat16)
    return (attended, layer_out)
```

```python
import jax
import jax.numpy as jnp
from jax import lax
from jax.sharding import PartitionSpec as P

QH = 16
KVH = 4


NEG_FLOOR = -1e30


def fold_block(carried, queries, key_rows, values, allowed, score_scale):
    running_max, running_sum, weighted = carried
    scores = (
        jnp.einsum("rhd,kd->rhk", queries, key_rows, preferred_element_type=jnp.float32)
        * score_scale
    )
    scores = jnp.where(allowed[:, None, :], scores, -jnp.inf)
    new_max = jnp.maximum(running_max, jnp.max(scores, axis=2))
    weights = jnp.exp(scores - new_max[:, :, None])
    shrink = jnp.exp(running_max - new_max)
    gathered = jnp.einsum(
        "rhk,kd->rhd", weights.astype(jnp.bfloat16), values, preferred_element_type=jnp.float32
    )
    return (
        new_max,
        running_sum * shrink + jnp.sum(weights, axis=2),
        weighted * shrink[:, :, None] + gathered,
    )


def body(
    query,
    suffix_kv,
    segment_ids,
    request_prefix,
    prefix_kv,
    shard_prefix,
    residual,
    out_weight,
    norm_gain,
    expert_ids,
    gate_weights,
    expert_in,
    expert_out,
):
    tok_rows = query.shape[0]
    head_size = suffix_kv.shape[3]
    heads_here = query.shape[1] // head_size
    kv_head = lax.axis_index("tensor") * heads_here // (QH // KVH)
    score_scale = head_size ** (-0.5)
    queries = query.reshape(tok_rows, heads_here, head_size)
    segments = segment_ids[0]
    requests = jnp.arange(request_prefix.shape[1], dtype=jnp.int32)
    row_prefix = jnp.sum(
        jnp.where(segments[:, None] == requests[None, :], request_prefix[0][None, :], 0), axis=1
    )
    blank_state = (
        jnp.full((tok_rows, heads_here), NEG_FLOOR, jnp.float32),
        jnp.zeros((tok_rows, heads_here), jnp.float32),
        jnp.zeros((tok_rows, heads_here, head_size), jnp.float32),
    )
    shard_len = prefix_kv.shape[0]
    own_cache = lax.dynamic_slice_in_dim(prefix_kv, kv_head, 1, 1).reshape(shard_len, 2 * head_size)
    cache_rows = lax.all_gather(own_cache, "seq", axis=0, tiled=True)
    owners = lax.all_gather(shard_prefix, "seq", axis=0, tiled=True)
    shard_count = owners.shape[0]
    shards = cache_rows.reshape(shard_count, -1, 2, head_size)

    def one_shard(inner_state, shard_item):
        block_rows, shard_owner = shard_item
        matching = row_prefix == shard_owner

        def attend(current):
            allowed = jnp.broadcast_to(matching[:, None], (tok_rows, block_rows.shape[0]))
            return fold_block(
                current, queries, block_rows[:, 0], block_rows[:, 1], allowed, score_scale
            )

        return (lax.cond(jnp.any(matching), attend, lambda current: current, inner_state), None)

    final_state, unused = lax.scan(one_shard, blank_state, (shards, owners))
    carried = final_state
    own_suffix = lax.dynamic_slice_in_dim(suffix_kv, kv_head, 1, 1).reshape(tok_rows, 2, head_size)
    positions = jnp.arange(tok_rows)
    causal = (segments[:, None] == segments[None, :]) & (positions[None, :] <= positions[:, None])
    carried = fold_block(carried, queries, own_suffix[:, 0], own_suffix[:, 1], causal, score_scale)
    running_max, running_sum, weighted = carried
    attention = (
        (weighted / running_sum[:, :, None])
        .reshape(tok_rows, heads_here * head_size)
        .astype(jnp.bfloat16)
    )
    projected = jnp.dot(attention, out_weight, preferred_element_type=jnp.float32)
    model_width = residual.shape[1]
    slice_width = model_width // lax.axis_size("tensor")
    first_col = lax.axis_index("tensor") * slice_width
    shared = lax.psum_scatter(
        projected.astype(jnp.bfloat16), "tensor", scatter_dimension=1, tiled=True
    )
    hidden_state = lax.dynamic_slice_in_dim(residual, first_col, slice_width, 1).astype(
        jnp.float32
    ) + shared.astype(jnp.float32)
    squares = lax.psum(jnp.sum(hidden_state * hidden_state, axis=1), "tensor")
    gain_cols = lax.dynamic_slice_in_dim(norm_gain, first_col, slice_width, 0)
    normed = (
        hidden_state * lax.rsqrt(squares / model_width + 1e-06)[:, None] * gain_cols[None, :]
    ).astype(jnp.bfloat16)
    attended = hidden_state.astype(jnp.bfloat16)
    exp_here = expert_in.shape[0]
    hid = expert_in.shape[3]
    experts = exp_here * lax.axis_size("seq")
    named = expert_ids[:, :, None] == jnp.arange(experts, dtype=jnp.int32)[None, None, :]
    gates = jnp.sum(jnp.where(named, gate_weights[:, :, None], 0.0), axis=1)
    all_gates = lax.all_gather(gates, "seq", axis=0, tiled=True)
    own_gates = lax.dynamic_slice_in_dim(all_gates, lax.axis_index("seq") * exp_here, exp_here, 1)
    rows = lax.all_gather(normed, "seq", axis=0, tiled=True)
    rows = lax.all_gather(rows, "tensor", axis=1, tiled=True)
    gate_up = jnp.einsum("rd,jdgh->rjgh", rows, expert_in, preferred_element_type=jnp.float32)
    hidden = jax.nn.silu(gate_up[:, :, 0]) * gate_up[:, :, 1] * own_gates[:, :, None]
    terms = jnp.dot(
        hidden.astype(jnp.bfloat16).reshape(-1, exp_here * hid),
        expert_out.reshape(exp_here * hid, model_width),
        preferred_element_type=jnp.float32,
    )
    summed = lax.psum_scatter(
        terms.astype(jnp.bfloat16), "tensor", scatter_dimension=1, tiled=True
    )
    mixture = lax.psum_scatter(summed, "seq", scatter_dimension=0, tiled=True)
    layer_out = (hidden_state + mixture.astype(jnp.float32)).astype(jnp.bfloat16)
    return (attended, layer_out)


def solution(mesh):
    in_specs = (
        P("seq", "tensor"),
        P("seq", None, None, None),
        P("seq", None),
        P("seq", None),
        P("seq", None, None, None),
        P("seq"),
        P("seq", None),
        P("tensor", None),
        P(),
        P("seq", None),
        P("seq", None),
        P("seq", None, None, "tensor"),
        P("seq", "tensor", None),
    )
    out_specs = (P("seq", "tensor"), P("seq", "tensor"))
    return jax.shard_map(body, mesh=mesh, in_specs=in_specs, out_specs=out_specs, check_vma=False)
```

```python
import functools

import jax
import jax.numpy as jnp
from jax import lax
from jax.experimental import pallas as pl
from jax.experimental.pallas import tpu as pltpu
from jax.sharding import PartitionSpec as P

QH = 16
KVH = 4


NEG_FLOOR = -1e30


def fold_block(carried, queries, key_rows, values, allowed, score_scale):
    running_max, running_sum, weighted = carried
    scores = (
        jnp.einsum("rhd,kd->rhk", queries, key_rows, preferred_element_type=jnp.float32)
        * score_scale
    )
    scores = jnp.where(allowed[:, None, :], scores, -jnp.inf)
    new_max = jnp.maximum(running_max, jnp.max(scores, axis=2))
    weights = jnp.exp(scores - new_max[:, :, None])
    shrink = jnp.exp(running_max - new_max)
    gathered = jnp.einsum(
        "rhk,kd->rhd", weights.astype(jnp.bfloat16), values, preferred_element_type=jnp.float32
    )
    return (
        new_max,
        running_sum * shrink + jnp.sum(weights, axis=2),
        weighted * shrink[:, :, None] + gathered,
    )


MESH = pl.DeviceIdType.MESH


def flipped(value, mask, bits):
    out = 0
    for b in range(bits):
        one = lax.rem(lax.div(value, 1 << b), 2)
        two = lax.rem(lax.div(mask, 1 << b), 2)
        out = out + (one + two - 2 * one * two) * (1 << b)
    return out


def moe_kernel(
    ns,
    nt,
    att,
    wo,
    res,
    gain,
    gates,
    win_hbm,
    wout_hbm,
    attended,
    layer,
    win,
    wout,
    hid,
    X,
    S,
    rc,
    rx,
    ry,
    rz,
    ps,
    pr,
    qs,
    qr,
    ls,
    p_s,
    p_r,
    q_s,
    q_r,
    z_s,
    z_r,
    y_s,
    y_r,
    x_s,
    x_r,
    c_s,
    c_r,
    oc_s,
    oc_r,
    ox_s,
    ox_r,
    oy_s,
    oy_r,
    oz_s,
    oz_r,
):
    rows, cols = res.shape
    nq, nx = ns // 2, nt // 2
    seq_bits, ten_bits = (ns - 1).bit_length(), (nt - 1).bit_length()
    s, t = lax.axis_index("seq"), lax.axis_index("tensor")
    i32 = jnp.int32

    def across_s(mask):
        return (flipped(s, i32(mask) if isinstance(mask, int) else mask, seq_bits), t)

    def across_t(mask):
        return (s, flipped(t, i32(mask), ten_bits))

    load_in = pltpu.make_async_copy(win_hbm, win, ls.at[0])
    load_out = pltpu.make_async_copy(wout_hbm, wout, ls.at[1])
    load_in.start()
    load_out.start()

    barrier = pltpu.get_barrier_semaphore()
    for k in range(1, nt):
        pl.semaphore_signal(barrier, inc=1, device_id=across_t(k), device_id_type=MESH)
    pl.semaphore_signal(barrier, inc=1, device_id=across_s(1), device_id_type=MESH)
    for q in range(1, nq):
        pl.semaphore_signal(barrier, inc=1, device_id=across_s(2 * q), device_id_type=MESH)
    pl.semaphore_wait(barrier, nt - 1 + nq)

    def move(src, dst, send, recv, dev):
        return pltpu.make_async_remote_copy(
            src_ref=src,
            dst_ref=dst,
            send_sem=send,
            recv_sem=recv,
            device_id=dev,
            device_id_type=MESH,
        )

    def both(q):
        return pl.ds(pl.multiple_of(q * 2 * rows, 2 * rows), 2 * rows)

    def half(q, pos):
        return pl.ds(pl.multiple_of((q * 2 + pos) * rows, rows), rows)

    def proj(k):
        return move(ps.at[k], pr.at[k], p_s.at[k], p_r.at[k], across_t(k))

    def sq(k):
        return move(qs, qr.at[k], q_s.at[k], q_r.at[k], across_t(k))

    def z_go(q):
        return move(
            X.at[0, half(0, 0)], X.at[0, half(q, 0)], z_s.at[q], z_r.at[q], across_s(2 * q)
        )

    def y_go(q):
        return move(
            X.at[0, half(q, 0)], X.at[0, half(q, 1)], y_s.at[q], y_r.at[q], across_s(1)
        )

    def x_go(q, a):
        return move(
            X.at[0, both(q)], X.at[2 * a, both(q)], x_s.at[q, a], x_r.at[q, a], across_t(2 * a)
        )

    def c_go(q, a):
        return move(
            X.at[2 * a, both(q)], X.at[2 * a + 1, both(q)], c_s.at[q, a], c_r.at[q, a], across_t(1)
        )

    def c_back(q, a):
        return move(
            S.at[2 * a + 1, both(q)], rc.at[a, both(q)], oc_s.at[q, a], oc_r.at[q, a], across_t(1)
        )

    def x_back(q, a):
        return move(
            S.at[2 * a, both(q)], rx.at[a - 1, both(q)], ox_s.at[q, a], ox_r.at[q, a], across_t(2 * a)
        )

    def y_back(q):
        return move(S.at[0, half(q, 1)], ry.at[q], oy_s.at[q], oy_r.at[q], across_s(1))

    def z_back(q):
        return move(S.at[0, half(q, 0)], rz.at[q], oz_s.at[q], oz_r.at[q], across_s(2 * q))

    def wide(k):
        return pl.ds(pl.multiple_of(flipped(t, i32(k), ten_bits) * cols, cols), cols)

    a_rows = att[...]
    for k in [*range(2, nt), 1]:
        ps[k] = jnp.dot(a_rows, wo[:, wide(k)], preferred_element_type=jnp.float32).astype(
            jnp.bfloat16
        )
        proj(k).start()
    total = res[...].astype(jnp.float32) + jnp.dot(
        a_rows, wo[:, wide(0)], preferred_element_type=jnp.float32
    )
    for k in range(1, nt):
        proj(k).wait_recv()
        total = total + pr[k].astype(jnp.float32)
    attended[...] = total.astype(jnp.bfloat16)
    hid[...] = total
    own_sq = jnp.sum(total * total, axis=1, keepdims=True)
    qs[...] = jnp.broadcast_to(own_sq, (rows, rows)).T[:8]
    for k in range(1, nt):
        sq(k).start()
    all_sq = qs[...]
    for k in range(1, nt):
        sq(k).wait_recv()
        all_sq = all_sq + qr[k]
    scale = lax.rsqrt(all_sq / (cols * nt) + 1e-06)
    scale = jnp.broadcast_to(scale[:1], (rows, rows)).T[:, :1]
    X[0, 0:rows, :] = (total * scale * gain[...]).astype(jnp.bfloat16)

    y_go(0).start()
    for q in range(1, nq):
        z_go(q).start()

    def spread_y(q, _):
        z_go(q).wait_recv()
        y_go(q).start()
        return 0

    lax.fori_loop(1, nq, spread_y, 0)

    def spread_x(q, _):
        y_go(q).wait_recv()
        for a in range(1, nx):
            x_go(q, a).start()
        c_go(q, 0).start()
        return 0

    lax.fori_loop(0, nq, spread_x, 0)
    load_in.wait()
    load_out.wait()

    def experts(q):
        for a in range(1, nx):
            x_go(q, a).wait_recv()
            c_go(q, a).start()
        up, gate = None, None
        for k in [*range(0, nt, 2), *range(1, nt, 2)]:
            if k % 2:
                c_go(q, k // 2).wait_recv()
            x = X[k, both(q), :]
            part = wide(k)
            g = jnp.dot(x, win[0, part, :], preferred_element_type=jnp.float32)
            u = jnp.dot(x, win[1, part, :], preferred_element_type=jnp.float32)
            gate = g if gate is None else gate + g
            up = u if up is None else up + u
        width = gate.shape[1]
        own = gates[both(q), :]
        each = width // own.shape[1]
        column = lax.broadcasted_iota(jnp.int32, gate.shape, 1)
        weight = own[:, 0:1]
        for j in range(1, own.shape[1]):
            weight = jnp.where(column >= j * each, own[:, j : j + 1], weight)
        hidden = (gate / (1.0 + jnp.exp(-gate)) * up * weight).astype(jnp.bfloat16)
        for k in [*range(1, nt, 2), *range(0, nt, 2)]:
            S[k, both(q), :] = jnp.dot(
                hidden, wout[:, wide(k)], preferred_element_type=jnp.float32
            ).astype(jnp.bfloat16)
            if k % 2:
                c_back(q, k // 2).start()

    def step(i, _):
        @pl.when(i < nq)
        def _():
            experts(i)

        @pl.when((i >= 1) & (i < nq + 1))
        def _():
            q = i - 1
            for a in [*range(1, nx), 0]:
                c_back(q, a).wait_recv()
                S[2 * a, both(q), :] = (
                    S[2 * a, both(q), :].astype(jnp.float32)
                    + rc[a, both(q), :].astype(jnp.float32)
                ).astype(jnp.bfloat16)
                if a:
                    x_back(q, a).start()

        @pl.when((i >= 2) & (i < nq + 2))
        def _():
            q = i - 2
            acc = S[0, both(q), :].astype(jnp.float32)
            for a in range(1, nx):
                x_back(q, a).wait_recv()
                acc = acc + rx[a - 1, both(q), :].astype(jnp.float32)
            S[0, both(q), :] = acc.astype(jnp.bfloat16)
            y_back(q).start()

        @pl.when(i >= 3)
        def _():
            q = i - 3
            y_back(q).wait_recv()
            S[0, half(q, 0), :] = (
                S[0, half(q, 0), :].astype(jnp.float32) + ry[q].astype(jnp.float32)
            ).astype(jnp.bfloat16)

            @pl.when(q > 0)
            def _():
                z_back(q).start()

        return 0

    lax.fori_loop(0, nq + 3, step, 0)
    out = hid[...] + S[0, half(0, 0), :].astype(jnp.float32)
    for q in range(1, nq):
        z_back(q).wait_recv()
        out = out + rz[q].astype(jnp.float32)
    layer[...] = out.astype(jnp.bfloat16)

    for k in range(1, nt):
        proj(k).wait_send()
        sq(k).wait_send()

    def drain(q, _):
        @pl.when(q > 0)
        def _():
            z_go(q).wait_send()
            z_back(q).wait_send()

        y_go(q).wait_send()
        y_back(q).wait_send()
        for a in range(nx):
            if a:
                x_go(q, a).wait_send()
                x_back(q, a).wait_send()
            c_go(q, a).wait_send()
            c_back(q, a).wait_send()
        return 0

    lax.fori_loop(0, nq, drain, 0)


def moe(ns, nt, att, wo, res, gain, gates, win, wout):
    rows, cols = res.shape
    nq, nx = ns // 2, nt // 2
    bf = jnp.bfloat16
    dma = pltpu.SemaphoreType.DMA
    vmem = pl.BlockSpec(memory_space=pltpu.VMEM)
    anywhere = pl.BlockSpec(memory_space=pl.ANY)
    everyone = ns * rows
    scratch = [
        pltpu.VMEM(win.shape, bf),
        pltpu.VMEM(wout.shape, bf),
        pltpu.VMEM((rows, cols), jnp.float32),
        pltpu.VMEM((nt, everyone, cols), bf),
        pltpu.VMEM((nt, everyone, cols), bf),
        pltpu.VMEM((nx, everyone, cols), bf),
        pltpu.VMEM((nx - 1, everyone, cols), bf),
        pltpu.VMEM((nq, rows, cols), bf),
        pltpu.VMEM((nq, rows, cols), bf),
        pltpu.VMEM((nt, rows, cols), bf),
        pltpu.VMEM((nt, rows, cols), bf),
        pltpu.VMEM((8, rows), jnp.float32),
        pltpu.VMEM((nt, 8, rows), jnp.float32),
        dma((2,)),
    ]
    for shape in [(nt,), (nt,), (nq,), (nq,), (nq, nx), (nq, nx), (nq, nx), (nq, nx), (nq,), (nq,)]:
        scratch += [dma(shape), dma(shape)]
    return pl.pallas_call(
        functools.partial(moe_kernel, ns, nt),
        out_shape=[jax.ShapeDtypeStruct((rows, cols), bf)] * 2,
        in_specs=[vmem] * 5 + [anywhere] * 2,
        out_specs=[vmem] * 2,
        scratch_shapes=scratch,
        compiler_params=pltpu.CompilerParams(
            collective_id=1, has_side_effects=True, vmem_limit_bytes=62 * 2**20
        ),
    )(att, wo, res, gain, gates, win, wout)


def body(
    query,
    suffix_kv,
    segment_ids,
    request_prefix,
    prefix_kv,
    shard_prefix,
    residual,
    out_weight,
    norm_gain,
    expert_ids,
    gate_weights,
    expert_in,
    expert_out,
):
    tok_rows = query.shape[0]
    head_size = suffix_kv.shape[3]
    heads_here = query.shape[1] // head_size
    kv_head = lax.axis_index("tensor") * heads_here // (QH // KVH)
    score_scale = head_size ** (-0.5)
    queries = query.reshape(tok_rows, heads_here, head_size)
    segments = segment_ids[0]
    requests = jnp.arange(request_prefix.shape[1], dtype=jnp.int32)
    row_prefix = jnp.sum(
        jnp.where(segments[:, None] == requests[None, :], request_prefix[0][None, :], 0), axis=1
    )
    blank_state = (
        jnp.full((tok_rows, heads_here), NEG_FLOOR, jnp.float32),
        jnp.zeros((tok_rows, heads_here), jnp.float32),
        jnp.zeros((tok_rows, heads_here, head_size), jnp.float32),
    )
    shard_len = prefix_kv.shape[0]
    own_cache = lax.dynamic_slice_in_dim(prefix_kv, kv_head, 1, 1).reshape(shard_len, 2 * head_size)
    cache_rows = lax.all_gather(own_cache, "seq", axis=0, tiled=True)
    exp_here = expert_in.shape[0]
    members = lax.axis_size("seq")
    experts = exp_here * members
    named = expert_ids[:, :, None] == jnp.arange(experts, dtype=jnp.int32)[None, None, :]
    gates = jnp.sum(jnp.where(named, gate_weights[:, :, None], 0.0), axis=1)
    owner_rows = jnp.broadcast_to(shard_prefix.astype(jnp.float32)[:, None], (8, experts))
    small = lax.all_gather(jnp.concatenate([gates, owner_rows], axis=0), "seq", axis=0)
    owners = small[:, tok_rows, 0].astype(jnp.int32)
    me = lax.axis_index("seq")
    own_gates = lax.dynamic_slice_in_dim(small[:, :tok_rows], me * exp_here, exp_here, 2)
    index = jnp.arange(members, dtype=jnp.int32)
    chosen = (index ^ me)[:, None] == index[None, :]
    own_gates = jnp.sum(jnp.where(chosen[:, :, None, None], own_gates[None], 0.0), axis=1)
    own_gates = own_gates.reshape(members * tok_rows, exp_here)
    shard_count = owners.shape[0]
    shards = cache_rows.reshape(shard_count, -1, 2, head_size)

    def one_shard(inner_state, shard_item):
        block_rows, shard_owner = shard_item
        matching = row_prefix == shard_owner

        def attend(current):
            allowed = jnp.broadcast_to(matching[:, None], (tok_rows, block_rows.shape[0]))
            return fold_block(
                current, queries, block_rows[:, 0], block_rows[:, 1], allowed, score_scale
            )

        return (lax.cond(jnp.any(matching), attend, lambda current: current, inner_state), None)

    final_state, unused = lax.scan(one_shard, blank_state, (shards, owners))
    carried = final_state
    own_suffix = lax.dynamic_slice_in_dim(suffix_kv, kv_head, 1, 1).reshape(tok_rows, 2, head_size)
    positions = jnp.arange(tok_rows)
    causal = (segments[:, None] == segments[None, :]) & (positions[None, :] <= positions[:, None])
    carried = fold_block(carried, queries, own_suffix[:, 0], own_suffix[:, 1], causal, score_scale)
    running_max, running_sum, weighted = carried
    attention = (
        (weighted / running_sum[:, :, None])
        .reshape(tok_rows, heads_here * head_size)
        .astype(jnp.bfloat16)
    )
    slice_width = query.shape[1]
    first_col = lax.axis_index("tensor") * slice_width
    width = exp_here * expert_in.shape[3]
    win = jnp.transpose(expert_in, (2, 1, 0, 3)).reshape(2, expert_in.shape[1], width)
    return tuple(
        moe(
            lax.axis_size("seq"),
            lax.axis_size("tensor"),
            attention,
            out_weight,
            lax.dynamic_slice_in_dim(residual, first_col, slice_width, 1),
            lax.dynamic_slice_in_dim(norm_gain, first_col, slice_width, 0)[None, :],
            own_gates,
            win,
            expert_out.reshape(width, expert_out.shape[2]),
        )
    )


def solution(mesh):
    in_specs = (
        P("seq", "tensor"),
        P("seq", None, None, None),
        P("seq", None),
        P("seq", None),
        P("seq", None, None, None),
        P("seq"),
        P("seq", None),
        P("tensor", None),
        P(),
        P("seq", None),
        P("seq", None),
        P("seq", None, None, "tensor"),
        P("seq", "tensor", None),
    )
    out_specs = (P("seq", "tensor"), P("seq", "tensor"))
    return jax.shard_map(body, mesh=mesh, in_specs=in_specs, out_specs=out_specs, check_vma=False)
```

```python
import functools

import jax
import jax.numpy as jnp
from jax import lax
from jax.experimental import pallas as pl
from jax.experimental.pallas import tpu as pltpu
from jax.sharding import PartitionSpec as P

QH = 16
KVH = 4


MESH = pl.DeviceIdType.MESH


def flipped(value, mask, bits):
    out = 0
    for b in range(bits):
        one = lax.rem(lax.div(value, 1 << b), 2)
        two = lax.rem(lax.div(mask, 1 << b), 2)
        out = out + (one + two - 2 * one * two) * (1 << b)
    return out


def moe_kernel(
    ns,
    nt,
    att,
    wo,
    res,
    gain,
    gates,
    win_hbm,
    wout_hbm,
    attended,
    layer,
    win,
    wout,
    hid,
    X,
    S,
    rc,
    rx,
    ry,
    rz,
    ps,
    pr,
    qs,
    qr,
    ls,
    p_s,
    p_r,
    q_s,
    q_r,
    z_s,
    z_r,
    y_s,
    y_r,
    x_s,
    x_r,
    c_s,
    c_r,
    oc_s,
    oc_r,
    ox_s,
    ox_r,
    oy_s,
    oy_r,
    oz_s,
    oz_r,
):
    rows, cols = res.shape
    nq, nx = ns // 2, nt // 2
    seq_bits, ten_bits = (ns - 1).bit_length(), (nt - 1).bit_length()
    s, t = lax.axis_index("seq"), lax.axis_index("tensor")
    i32 = jnp.int32

    def across_s(mask):
        return (flipped(s, i32(mask) if isinstance(mask, int) else mask, seq_bits), t)

    def across_t(mask):
        return (s, flipped(t, i32(mask), ten_bits))

    load_in = pltpu.make_async_copy(win_hbm, win, ls.at[0])
    load_out = pltpu.make_async_copy(wout_hbm, wout, ls.at[1])
    load_in.start()
    load_out.start()

    barrier = pltpu.get_barrier_semaphore()
    for k in range(1, nt):
        pl.semaphore_signal(barrier, inc=1, device_id=across_t(k), device_id_type=MESH)
    pl.semaphore_signal(barrier, inc=1, device_id=across_s(1), device_id_type=MESH)
    for q in range(1, nq):
        pl.semaphore_signal(barrier, inc=1, device_id=across_s(2 * q), device_id_type=MESH)
    pl.semaphore_wait(barrier, nt - 1 + nq)

    def move(src, dst, send, recv, dev):
        return pltpu.make_async_remote_copy(
            src_ref=src,
            dst_ref=dst,
            send_sem=send,
            recv_sem=recv,
            device_id=dev,
            device_id_type=MESH,
        )

    def both(q):
        return pl.ds(pl.multiple_of(q * 2 * rows, 2 * rows), 2 * rows)

    def half(q, pos):
        return pl.ds(pl.multiple_of((q * 2 + pos) * rows, rows), rows)

    def proj(k):
        return move(ps.at[k], pr.at[k], p_s.at[k], p_r.at[k], across_t(k))

    def sq(k):
        return move(qs, qr.at[k], q_s.at[k], q_r.at[k], across_t(k))

    def z_go(q):
        return move(
            X.at[0, half(0, 0)], X.at[0, half(q, 0)], z_s.at[q], z_r.at[q], across_s(2 * q)
        )

    def y_go(q):
        return move(
            X.at[0, half(q, 0)], X.at[0, half(q, 1)], y_s.at[q], y_r.at[q], across_s(1)
        )

    def x_go(q, a):
        return move(
            X.at[0, both(q)], X.at[2 * a, both(q)], x_s.at[q, a], x_r.at[q, a], across_t(2 * a)
        )

    def c_go(q, a):
        return move(
            X.at[2 * a, both(q)], X.at[2 * a + 1, both(q)], c_s.at[q, a], c_r.at[q, a], across_t(1)
        )

    def c_back(q, a):
        return move(
            S.at[2 * a + 1, both(q)], rc.at[a, both(q)], oc_s.at[q, a], oc_r.at[q, a], across_t(1)
        )

    def x_back(q, a):
        return move(
            S.at[2 * a, both(q)], rx.at[a - 1, both(q)], ox_s.at[q, a], ox_r.at[q, a], across_t(2 * a)
        )

    def y_back(q):
        return move(S.at[0, half(q, 1)], ry.at[q], oy_s.at[q], oy_r.at[q], across_s(1))

    def z_back(q):
        return move(S.at[0, half(q, 0)], rz.at[q], oz_s.at[q], oz_r.at[q], across_s(2 * q))

    def wide(k):
        return pl.ds(pl.multiple_of(flipped(t, i32(k), ten_bits) * cols, cols), cols)

    a_rows = att[...]
    for k in [*range(2, nt), 1]:
        ps[k] = jnp.dot(a_rows, wo[:, wide(k)], preferred_element_type=jnp.float32).astype(
            jnp.bfloat16
        )
        proj(k).start()
    total = res[...].astype(jnp.float32) + jnp.dot(
        a_rows, wo[:, wide(0)], preferred_element_type=jnp.float32
    )
    for k in range(1, nt):
        proj(k).wait_recv()
        total = total + pr[k].astype(jnp.float32)
    attended[...] = total.astype(jnp.bfloat16)
    hid[...] = total
    own_sq = jnp.sum(total * total, axis=1, keepdims=True)
    qs[...] = jnp.broadcast_to(own_sq, (rows, rows)).T[:8]
    for k in range(1, nt):
        sq(k).start()
    all_sq = qs[...]
    for k in range(1, nt):
        sq(k).wait_recv()
        all_sq = all_sq + qr[k]
    scale = lax.rsqrt(all_sq / (cols * nt) + 1e-06)
    scale = jnp.broadcast_to(scale[:1], (rows, rows)).T[:, :1]
    X[0, 0:rows, :] = (total * scale * gain[...]).astype(jnp.bfloat16)

    y_go(0).start()
    for q in range(1, nq):
        z_go(q).start()

    def spread_y(q, _):
        z_go(q).wait_recv()
        y_go(q).start()
        return 0

    lax.fori_loop(1, nq, spread_y, 0)

    def spread_x(q, _):
        y_go(q).wait_recv()
        for a in range(1, nx):
            x_go(q, a).start()
        c_go(q, 0).start()
        return 0

    lax.fori_loop(0, nq, spread_x, 0)
    load_in.wait()
    load_out.wait()

    def experts(q):
        for a in range(1, nx):
            x_go(q, a).wait_recv()
            c_go(q, a).start()
        up, gate = None, None
        for k in [*range(0, nt, 2), *range(1, nt, 2)]:
            if k % 2:
                c_go(q, k // 2).wait_recv()
            x = X[k, both(q), :]
            part = wide(k)
            g = jnp.dot(x, win[0, part, :], preferred_element_type=jnp.float32)
            u = jnp.dot(x, win[1, part, :], preferred_element_type=jnp.float32)
            gate = g if gate is None else gate + g
            up = u if up is None else up + u
        width = gate.shape[1]
        own = gates[both(q), :]
        each = width // own.shape[1]
        column = lax.broadcasted_iota(jnp.int32, gate.shape, 1)
        weight = own[:, 0:1]
        for j in range(1, own.shape[1]):
            weight = jnp.where(column >= j * each, own[:, j : j + 1], weight)
        hidden = (gate / (1.0 + jnp.exp(-gate)) * up * weight).astype(jnp.bfloat16)
        for k in [*range(1, nt, 2), *range(0, nt, 2)]:
            S[k, both(q), :] = jnp.dot(
                hidden, wout[:, wide(k)], preferred_element_type=jnp.float32
            ).astype(jnp.bfloat16)
            if k % 2:
                c_back(q, k // 2).start()

    def step(i, _):
        @pl.when(i < nq)
        def _():
            experts(i)

        @pl.when((i >= 1) & (i < nq + 1))
        def _():
            q = i - 1
            for a in [*range(1, nx), 0]:
                c_back(q, a).wait_recv()
                S[2 * a, both(q), :] = (
                    S[2 * a, both(q), :].astype(jnp.float32)
                    + rc[a, both(q), :].astype(jnp.float32)
                ).astype(jnp.bfloat16)
                if a:
                    x_back(q, a).start()

        @pl.when((i >= 2) & (i < nq + 2))
        def _():
            q = i - 2
            acc = S[0, both(q), :].astype(jnp.float32)
            for a in range(1, nx):
                x_back(q, a).wait_recv()
                acc = acc + rx[a - 1, both(q), :].astype(jnp.float32)
            S[0, both(q), :] = acc.astype(jnp.bfloat16)
            y_back(q).start()

        @pl.when(i >= 3)
        def _():
            q = i - 3
            y_back(q).wait_recv()
            S[0, half(q, 0), :] = (
                S[0, half(q, 0), :].astype(jnp.float32) + ry[q].astype(jnp.float32)
            ).astype(jnp.bfloat16)

            @pl.when(q > 0)
            def _():
                z_back(q).start()

        return 0

    lax.fori_loop(0, nq + 3, step, 0)
    out = hid[...] + S[0, half(0, 0), :].astype(jnp.float32)
    for q in range(1, nq):
        z_back(q).wait_recv()
        out = out + rz[q].astype(jnp.float32)
    layer[...] = out.astype(jnp.bfloat16)

    for k in range(1, nt):
        proj(k).wait_send()
        sq(k).wait_send()

    def drain(q, _):
        @pl.when(q > 0)
        def _():
            z_go(q).wait_send()
            z_back(q).wait_send()

        y_go(q).wait_send()
        y_back(q).wait_send()
        for a in range(nx):
            if a:
                x_go(q, a).wait_send()
                x_back(q, a).wait_send()
            c_go(q, a).wait_send()
            c_back(q, a).wait_send()
        return 0

    lax.fori_loop(0, nq, drain, 0)


def moe(ns, nt, att, wo, res, gain, gates, win, wout):
    rows, cols = res.shape
    nq, nx = ns // 2, nt // 2
    bf = jnp.bfloat16
    dma = pltpu.SemaphoreType.DMA
    vmem = pl.BlockSpec(memory_space=pltpu.VMEM)
    anywhere = pl.BlockSpec(memory_space=pl.ANY)
    everyone = ns * rows
    scratch = [
        pltpu.VMEM(win.shape, bf),
        pltpu.VMEM(wout.shape, bf),
        pltpu.VMEM((rows, cols), jnp.float32),
        pltpu.VMEM((nt, everyone, cols), bf),
        pltpu.VMEM((nt, everyone, cols), bf),
        pltpu.VMEM((nx, everyone, cols), bf),
        pltpu.VMEM((nx - 1, everyone, cols), bf),
        pltpu.VMEM((nq, rows, cols), bf),
        pltpu.VMEM((nq, rows, cols), bf),
        pltpu.VMEM((nt, rows, cols), bf),
        pltpu.VMEM((nt, rows, cols), bf),
        pltpu.VMEM((8, rows), jnp.float32),
        pltpu.VMEM((nt, 8, rows), jnp.float32),
        dma((2,)),
    ]
    for shape in [(nt,), (nt,), (nq,), (nq,), (nq, nx), (nq, nx), (nq, nx), (nq, nx), (nq,), (nq,)]:
        scratch += [dma(shape), dma(shape)]
    return pl.pallas_call(
        functools.partial(moe_kernel, ns, nt),
        out_shape=[jax.ShapeDtypeStruct((rows, cols), bf)] * 2,
        in_specs=[vmem] * 5 + [anywhere] * 2,
        out_specs=[vmem] * 2,
        scratch_shapes=scratch,
        compiler_params=pltpu.CompilerParams(
            collective_id=1, has_side_effects=True, vmem_limit_bytes=62 * 2**20
        ),
    )(att, wo, res, gain, gates, win, wout)


def attend_kernel(
    keys, scale, owners, needed, query, row_prefix, cache, suffix, causal, out, top, total, acc
):
    size = suffix.shape[1] // 2
    heads = query.shape[1] // size
    tokens = query.shape[0]
    q = jnp.concatenate([query[:, h * size : (h + 1) * size] for h in range(heads)], axis=0)
    spot = pl.program_id(0)

    def scores_of(k):
        return (
            lax.dot_general(q, k, (((1,), (1,)), ((), ())), preferred_element_type=jnp.float32)
            * scale
        )

    @pl.when(spot == 0)
    def _():
        seen = jnp.concatenate([causal[...]] * heads, axis=0) > 0.5
        scores = jnp.where(seen, scores_of(suffix[:, :size]), -jnp.inf)
        high = jnp.max(scores, axis=1, keepdims=True)
        weights = jnp.exp(scores - high)
        top[...] = high
        total[...] = jnp.sum(weights, axis=1, keepdims=True)
        acc[...] = jnp.dot(
            weights.astype(jnp.bfloat16), suffix[:, size:], preferred_element_type=jnp.float32
        )

    @pl.when(needed[spot] > 0)
    def _():
        match = row_prefix[...] == owners[spot]
        scores = jnp.where(match, scores_of(cache[0, :keys, :size]), -jnp.inf)
        high = jnp.maximum(top[...], jnp.max(scores, axis=1, keepdims=True))
        weights = jnp.exp(scores - high)
        shrink = jnp.exp(top[...] - high)
        top[...] = high
        total[...] = total[...] * shrink + jnp.sum(weights, axis=1, keepdims=True)
        acc[...] = acc[...] * shrink + jnp.dot(
            weights.astype(jnp.bfloat16),
            cache[0, :keys, size:],
            preferred_element_type=jnp.float32,
        )

    @pl.when(spot == pl.num_programs(0) - 1)
    def _():
        result = (acc[...] / total[...]).astype(jnp.bfloat16)
        for h in range(heads):
            out[:, h * size : (h + 1) * size] = result[h * tokens : (h + 1) * tokens]


def attend(keys, scale, owners, needed, query, row_prefix, cache, suffix, causal):
    heads = query.shape[1] * 2 // suffix.shape[1]
    lines = heads * query.shape[0]
    smem = pl.BlockSpec(memory_space=pltpu.SMEM)
    vmem = pl.BlockSpec(memory_space=pltpu.VMEM)
    return pl.pallas_call(
        functools.partial(attend_kernel, keys, scale),
        grid=(cache.shape[0],),
        out_shape=jax.ShapeDtypeStruct(query.shape, jnp.bfloat16),
        in_specs=[
            smem,
            smem,
            vmem,
            vmem,
            pl.BlockSpec((1, cache.shape[1], cache.shape[2]), lambda i: (i, 0, 0)),
            vmem,
            vmem,
        ],
        out_specs=vmem,
        scratch_shapes=[
            pltpu.VMEM((lines, 1), jnp.float32),
            pltpu.VMEM((lines, 1), jnp.float32),
            pltpu.VMEM((lines, suffix.shape[1] // 2), jnp.float32),
        ],
        compiler_params=pltpu.CompilerParams(vmem_limit_bytes=48 * 2**20),
    )(owners, needed, query, row_prefix, cache, suffix, causal)


def body(
    query,
    suffix_kv,
    segment_ids,
    request_prefix,
    prefix_kv,
    shard_prefix,
    residual,
    out_weight,
    norm_gain,
    expert_ids,
    gate_weights,
    expert_in,
    expert_out,
):
    tok_rows = query.shape[0]
    head_size = suffix_kv.shape[3]
    heads_here = query.shape[1] // head_size
    kv_head = lax.axis_index("tensor") * heads_here // (QH // KVH)
    score_scale = head_size ** (-0.5)
    segments = segment_ids[0]
    requests = jnp.arange(request_prefix.shape[1], dtype=jnp.int32)
    row_prefix = jnp.sum(
        jnp.where(segments[:, None] == requests[None, :], request_prefix[0][None, :], 0), axis=1
    )
    shard_len = prefix_kv.shape[0]
    exp_here = expert_in.shape[0]
    members = lax.axis_size("seq")
    experts = exp_here * members
    named = expert_ids[:, :, None] == jnp.arange(experts, dtype=jnp.int32)[None, None, :]
    gates = jnp.sum(jnp.where(named, gate_weights[:, :, None], 0.0), axis=1)
    gate_rows = gates.astype(jnp.bfloat16).reshape(-1, 2 * head_size)
    owner_rows = jnp.broadcast_to(shard_prefix.astype(jnp.bfloat16)[:, None], (8, 2 * head_size))
    own_cache = lax.dynamic_slice_in_dim(prefix_kv, kv_head, 1, 1).reshape(shard_len, 2 * head_size)
    packed = jnp.concatenate([own_cache, owner_rows, gate_rows], axis=0)
    cache = lax.all_gather(packed, "seq", axis=0, tiled=True)
    cache = cache.reshape(members, packed.shape[0], 2 * head_size)
    owners = cache[:, shard_len, 0].astype(jnp.int32)
    small = cache[:, shard_len + 8 :].astype(jnp.float32).reshape(members, tok_rows, experts)
    me = lax.axis_index("seq")
    index = jnp.arange(members, dtype=jnp.int32)
    own_gates = lax.dynamic_slice_in_dim(small, me * exp_here, exp_here, 2)
    chosen = (index ^ me)[:, None] == index[None, :]
    own_gates = jnp.sum(jnp.where(chosen[:, :, None, None], own_gates[None], 0.0), axis=1)
    own_gates = own_gates.reshape(members * tok_rows, exp_here)
    needed = jnp.any(owners[:, None] == row_prefix[None, :], axis=1).astype(jnp.int32)
    own_suffix = lax.dynamic_slice_in_dim(suffix_kv, kv_head, 1, 1).reshape(
        tok_rows, 2 * head_size
    )
    positions = jnp.arange(tok_rows)
    causal = (segments[:, None] == segments[None, :]) & (positions[None, :] <= positions[:, None])
    attention = attend(
        shard_len,
        score_scale,
        owners,
        needed,
        query,
        jnp.tile(row_prefix[:, None], (heads_here, 1)),
        cache,
        own_suffix,
        causal.astype(jnp.float32),
    )
    slice_width = query.shape[1]
    first_col = lax.axis_index("tensor") * slice_width
    width = exp_here * expert_in.shape[3]
    win = jnp.transpose(expert_in, (2, 1, 0, 3)).reshape(2, expert_in.shape[1], width)
    return tuple(
        moe(
            lax.axis_size("seq"),
            lax.axis_size("tensor"),
            attention,
            out_weight,
            lax.dynamic_slice_in_dim(residual, first_col, slice_width, 1),
            lax.dynamic_slice_in_dim(norm_gain, first_col, slice_width, 0)[None, :],
            own_gates,
            win,
            expert_out.reshape(width, expert_out.shape[2]),
        )
    )


def solution(mesh):
    in_specs = (
        P("seq", "tensor"),
        P("seq", None, None, None),
        P("seq", None),
        P("seq", None),
        P("seq", None, None, None),
        P("seq"),
        P("seq", None),
        P("tensor", None),
        P(),
        P("seq", None),
        P("seq", None),
        P("seq", None, None, "tensor"),
        P("seq", "tensor", None),
    )
    out_specs = (P("seq", "tensor"), P("seq", "tensor"))
    return jax.shard_map(body, mesh=mesh, in_specs=in_specs, out_specs=out_specs, check_vma=False)
```
